256 devices in a mesh: section: 2 (over core), expert: 128 (over x, z, y).
Axes of the slice: x: 4, y: 4, z: 8, core: 2. Of those that a mesh axis runs over, the one named last changes fastest.
Arguments:
- arriving: bfloat16 [2, 8192, 7168], P('section', 'expert'), may hold values from -6 to 6
- gains: float32 [2, 7168], P('section'), may hold values from 0.5 to 2
- routes: int32 [2, 8192, 3], P('section', 'expert'), may hold values from 0 to 31, all different within a row; in each aligned block of 64 rows (0 to 63, 64 to 127, ..., all dimensions but the last counted through in order) at most 7 rows name the same one
- combine_weight: float32 [2, 8192, 3], P('section', 'expert'), may hold values from 0.2 to 1
- gate_weight: bfloat16 [2, 7168, 32768], P('section', None, 'expert'), may hold values from -0.0625 to 0.0625
- up_weight: bfloat16 [2, 7168, 32768], P('section', None, 'expert'), may hold values from -0.0625 to 0.0625
- down_weight: bfloat16 [2, 32768, 7168], P('section', 'expert'), may hold values from -0.1875 to 0.1875
Outputs:
- moved: bfloat16 [2, 8192, 7168], P('section', 'expert')
The draws below stay inside these ranges and needn't reach their ends.
Inputs may be any that keep to these rules, and one draw needn't show every extreme that they name: `routes`: A token names 3 different experts. Among the tokens of one device (aligned blocks of 64 rows), no expert is named by more than 7 of them, and in every draw some expert is named by exactly 7 of them in some device's rows.
All inputs are finite; a program needn't handle non-finite values.
Results may differ from the reference program's by a relative error of at most 0.0095.
Values may be sent and summed in bfloat16 or wider, within the bound.
No kernel may reach another device: no remote copies, remote signals or barrier semaphores. Data moves between devices by JAX's collectives and lax.ppermute only.
A program may use at most 128 MiB of HBM per device.

```python
import math
import jax
import jax.numpy as jnp
import numpy as np
from jax import lax

D = 7168
FF_WIN = 1024
HID_DEV = 256
TOP = 3
TOK_DEV = 64
SECTIONS = 2
SPLIT = 4
EXPERTS = 32
CAP = 7
TOKENS = 8192
N_EXPERT = 128


def steps_of(stream_key, dims, split, least, high):
    level = 1.0
    for dim, parts in split:
        draws = jax.random.uniform(jax.random.fold_in(jax.random.fold_in(stream_key, 6), dim), (parts,), jnp.float32, least / len(split), high / len(split))
        level = level * jnp.repeat(jnp.exp(draws), dims[dim] // parts).reshape((-1,) + (1,) * (len(dims) - 1 - dim))
    return level


def assign_block(stream_key, own, number, rows, number_of, top, limit, lean):
    order = jax.random.permutation(stream_key, number_of)
    crowded, usual = shares(number_of, rows * top, limit, lean, True), shares(number_of, rows * top, limit, lean, False)
    places = jnp.arange(number_of)

    def named(tallies, offset_by):
        used = int((tallies > 0).sum())
        fixed = max(1, used // 4)
        shifted = fixed + (places - fixed + offset_by * (used - fixed)) % max(1, number_of - fixed)
        return jnp.zeros((number_of,), jnp.int32).at[order[jnp.where(places < fixed, places, shifted)]].set(jnp.asarray(tallies, jnp.int32))

    tallies = jnp.where(number % 4 == 0, named(crowded, number // 4), named(usual, number - number // 4 - 1))
    mixed = jax.random.permutation(jax.random.fold_in(own, 3), number_of)
    donor, receiver = mixed[0:number_of // 2 * 2:2], mixed[1:number_of // 2 * 2:2]
    room = jnp.minimum(tallies[donor] - 1, limit - tallies[receiver]) // 2
    room = jnp.where((donor == order[0]) | (receiver == order[0]) | (tallies[receiver] == 0), 0, jnp.maximum(room, 0))
    shifted = jax.random.randint(jax.random.fold_in(own, 4), (number_of // 2,), 0, 1 << 20) % (room + 1)
    tallies = tallies.at[donor].add(-shifted).at[receiver].add(shifted)
    members = jnp.searchsorted(jnp.cumsum(tallies), jnp.arange(rows * top), side="right").astype(jnp.int32)
    table = members.reshape(top, rows).T
    table = table[jax.random.permutation(jax.random.fold_in(own, 1), rows)]
    offset_by = jax.random.randint(jax.random.fold_in(own, 2), (rows, 1), 0, top)
    return jnp.take_along_axis(table, (jnp.arange(top)[None, :] + offset_by) % top, axis=1)


def shares(count, total, bound, slope, full):
    portions = [(1 << 20) // math.isqrt(rank ** slope) + 1 for rank in range(1, count + 1)]
    largest = bound if full else min(bound, max(-(-total // count), total * portions[0] // sum(portions)))
    least = 1 if total - largest >= count - 1 else 0
    given, surplus = [largest] + [least] * (count - 1), total - largest - least * (count - 1)
    while surplus > 0:
        candidates = [i for i in range(1, count) if given[i] < largest] or [i for i in range(1, count) if given[i] < bound]
        pool, budget = sum([portions[i] for i in candidates]), surplus
        for i in candidates:
            addition = min(bound - given[i], max(1, budget * portions[i] // pool), surplus)
            given[i] = given[i] + addition
            surplus = surplus - addition
    return np.array(given)


def noise(rng, shape, width, reach, cuts=(), kind=jnp.bfloat16):
    drawn = width * jax.random.normal(rng, shape, jnp.float32)
    if cuts:
        drawn = drawn * steps_of(rng, shape, cuts, -0.22, 0.18)
    return jnp.clip(drawn, -reach, reach).astype(kind)


def setup_inputs(seed: int = 0) -> dict:
    arg_keys = jax.random.split(jax.random.key(seed), 8)
    arriving = noise(arg_keys[0], (SECTIONS, TOKENS, D), 1.0, 6.0, ((0, 2), (1, 128)))
    gains = jnp.clip(jnp.exp(math.log(2.0) - 1.3862944 * jax.random.uniform(arg_keys[1], (SECTIONS, D), jnp.float32) ** steps_of(arg_keys[1], (SECTIONS, D), ((0, 2),), -0.2, 0.2)), 0.5, 2.0)
    routes_keys = jax.random.split(jax.random.fold_in(arg_keys[2], 1), SECTIONS * TOKENS // TOK_DEV)
    routes_turns = jax.random.permutation(jax.random.fold_in(arg_keys[2], 3), SECTIONS * TOKENS // TOK_DEV)
    routes = jax.vmap(lambda own, number: assign_block(jax.random.fold_in(arg_keys[2], 2), own, number, TOK_DEV, EXPERTS, TOP, CAP, 2))(routes_keys, routes_turns).reshape((SECTIONS, TOKENS, TOP))
    combine_weight = jnp.clip(0.2 + 0.8 * jax.random.uniform(arg_keys[3], (SECTIONS, TOKENS, TOP), jnp.float32) ** steps_of(arg_keys[3], (SECTIONS, TOKENS, TOP), ((0, 2), (1, 128)), -0.2, 0.2), 0.2, 1.0)
    gate_weight = noise(arg_keys[4], (SECTIONS, D, EXPERTS * FF_WIN), D ** -0.5, 0.0625, ((0, 2), (2, 128)))
    up_weight = noise(arg_keys[5], (SECTIONS, D, EXPERTS * FF_WIN), D ** -0.5, 0.0625, ((0, 2), (2, 128)))
    down_weight = noise(arg_keys[6], (SECTIONS, EXPERTS * FF_WIN, D), FF_WIN ** -0.5, 0.1875, ((0, 2), (1, 128)))
    return dict(arriving=arriving, gains=gains, routes=routes, combine_weight=combine_weight, gate_weight=gate_weight, up_weight=up_weight, down_weight=down_weight)


epsilon = 1e-06

def reference(arriving, gains, routes, combine_weight, gate_weight, up_weight, down_weight):
    results = []
    for section_index in range(SECTIONS):
        inbound = arriving[(section_index - 1) % SECTIONS]
        widened = inbound.astype(jnp.float32)
        inv_rms = lax.rsqrt(lax.optimization_barrier(jnp.mean(widened * widened, axis=-1, keepdims=True)) + epsilon)
        normed = (widened * inv_rms * gains[section_index][None, :]).astype(jnp.bfloat16)
        chosen = routes[section_index].reshape(N_EXPERT, TOK_DEV * TOP).astype(jnp.int32)
        expert_ids = jnp.arange(EXPERTS, dtype=jnp.int32)
        onehot = (chosen[:, :, None] == expert_ids[None, None, :]).astype(jnp.int32)
        earlier = jnp.cumsum(onehot, axis=1) - onehot
        slot_index = lax.optimization_barrier(jnp.sum(earlier * onehot, axis=2)).astype(jnp.int32)
        source_ids = jnp.broadcast_to(jnp.arange(N_EXPERT, dtype=jnp.int32)[:, None], chosen.shape)
        local_ids = jnp.broadcast_to((jnp.arange(TOK_DEV * TOP, dtype=jnp.int32) // TOP)[None, :], chosen.shape)
        token_ids = (source_ids * TOK_DEV + local_ids).astype(jnp.int32)
        positions = (chosen * (N_EXPERT * CAP) + source_ids * CAP + slot_index).reshape(-1).astype(jnp.int32)
        row_table = jnp.zeros((EXPERTS * N_EXPERT * CAP,), jnp.int32).at[positions].set(token_ids.reshape(-1))
        slot_weights = jnp.zeros((EXPERTS * N_EXPERT * CAP,), jnp.float32).at[positions].set(combine_weight[section_index].reshape(-1).astype(jnp.float32))
        row_table = row_table.reshape(EXPERTS, N_EXPERT * CAP)
        slot_weights = slot_weights.reshape(EXPERTS, N_EXPERT * CAP)
        gate_all = gate_weight[section_index]
        up_all = up_weight[section_index]
        down_all = down_weight[section_index]

        def visit(combined, expert_id):
            gathered = normed[row_table[expert_id]]
            start = (expert_id * FF_WIN).astype(jnp.int32)
            gate_cols = lax.dynamic_slice_in_dim(gate_all, start, FF_WIN, 1)
            up_cols = lax.dynamic_slice_in_dim(up_all, start, FF_WIN, 1)
            down_rows = lax.dynamic_slice_in_dim(down_all, start, FF_WIN, 0)
            accum = jnp.zeros((N_EXPERT * CAP, D), jnp.float32)
            for shard_id in range(SPLIT):
                lower = shard_id * HID_DEV
                gate_act = jnp.dot(gathered, gate_cols[:, lower:lower + HID_DEV], preferred_element_type=jnp.float32)
                up_act = jnp.dot(gathered, up_cols[:, lower:lower + HID_DEV], preferred_element_type=jnp.float32)
                hidden = (jax.nn.silu(gate_act) * up_act).astype(jnp.bfloat16)
                partial_value = jnp.dot(hidden, down_rows[lower:lower + HID_DEV, :], preferred_element_type=jnp.float32)
                accum = accum + partial_value.astype(jnp.bfloat16).astype(jnp.float32)
            expert_out = accum.astype(jnp.bfloat16).astype(jnp.float32)
            combined = combined.at[row_table[expert_id]].add(slot_weights[expert_id][:, None] * expert_out)
            return (combined, None)
        combined, _ = lax.scan(visit, jnp.zeros((TOKENS, D), jnp.float32), jnp.arange(EXPERTS, dtype=jnp.int32))
        results.append((widened + combined).astype(jnp.bfloat16))
    return jnp.stack(results, axis=0)
```

```python
import jax
import jax.numpy as jnp
from jax import lax
from jax.sharding import PartitionSpec as P

FF_WIN = 1024
HID_DEV = 256
CHUNKS = 4

epsilon = 1e-06


def body(arriving, gains, routes, combine_weight, gate_weight, up_weight, down_weight):
    device_count = lax.axis_size("expert")
    ring = FF_WIN // HID_DEV
    experts = device_count // ring
    tok_count = arriving.shape[1]
    feature_count = arriving.shape[2]
    top_count = routes.shape[2]
    capacity = min(tok_count, 5 * tok_count * top_count // (4 * experts))
    slots = experts * capacity
    half = slots // 2
    width = feature_count // CHUNKS
    planes = [[g * ring + r for g in range(experts)] for r in range(ring)]

    def shift(block, step):
        route = [(i, i - i % ring + (i + step) % ring) for i in range(device_count)]
        return lax.ppermute(block, "expert", route)

    def exchange(block):
        return lax.all_to_all(
            block, "expert", split_axis=0, concat_axis=0, axis_index_groups=planes, tiled=True
        )

    other = [(i, 1 - i) for i in range(2)]
    inbound = lax.ppermute(arriving, "section", other)[0]
    widened = inbound.astype(jnp.float32)
    inv_rms = lax.rsqrt(jnp.mean(widened * widened, axis=-1, keepdims=True) + epsilon)
    normed = (widened * inv_rms * gains[0][None, :]).astype(jnp.bfloat16)
    chosen = routes[0].reshape(-1)
    onehot = (chosen[:, None] == jnp.arange(experts, dtype=jnp.int32)[None, :]).astype(jnp.int32)
    earlier = jnp.cumsum(onehot, axis=0) - onehot
    slot_index = jnp.sum(earlier * onehot, axis=1)
    target = (chosen * capacity + slot_index).reshape(tok_count, top_count)
    slot_ids = jnp.arange(slots, dtype=jnp.int32)
    hits = target[:, :, None] == slot_ids[None, None, :]
    placement = jnp.any(hits, axis=1).astype(jnp.bfloat16).T
    mixing = jnp.sum(jnp.where(hits, combine_weight[0][:, :, None], 0.0), axis=1)
    mix_high = lax.reduce_precision(mixing, 8, 7)
    mix_low = (mixing - mix_high).astype(jnp.bfloat16)
    mix_high = mix_high.astype(jnp.bfloat16)

    gate_act = up_act = None
    weights = jnp.concatenate([gate_weight[0], up_weight[0]], axis=1)
    total = None
    for c in range(CHUNKS):
        cols = slice(c * width, (c + 1) * width)
        packed = jnp.dot(placement, normed[:, cols], preferred_element_type=jnp.float32)
        packed = packed.astype(jnp.bfloat16).reshape(experts, capacity, width)
        own = exchange(packed).reshape(slots, width)
        first, second = own[:half], own[half:]
        left_first, right_second = shift(first, 1), shift(second, -1)
        left_second, right_first = shift(second, 1), shift(first, -1)
        far_first, far_second = shift(left_first, 1), shift(right_second, -1)
        rows = jnp.concatenate(
            [far_first, far_second, left_first, left_second, right_first, right_second, own], axis=0
        )
        term = jnp.dot(rows, weights[cols], preferred_element_type=jnp.float32)
        total = term if total is None else total + term
    hidden = (jax.nn.silu(total[:, :HID_DEV]) * total[:, HID_DEV:]).astype(jnp.bfloat16)

    results = []
    for c in range(CHUNKS):
        cols = slice(c * width, (c + 1) * width)
        part = jnp.dot(hidden, down_weight[0][:, cols], preferred_element_type=jnp.float32)
        part = part.astype(jnp.bfloat16)
        pieces = [part[i * half : (i + 1) * half] for i in range(8)]
        far_first, far_second, left_first, left_second, right_first, right_second = pieces[:6]
        from_left, from_right = shift(far_second, 1), shift(far_first, -1)
        direct_first, direct_second = shift(right_first, 1), shift(left_second, -1)
        summed_second = shift(right_second + from_left, 1)
        summed_first = shift(left_first + from_right, -1)
        arrived_left = jnp.concatenate([direct_first, summed_second], axis=0)
        arrived_right = jnp.concatenate([summed_first, direct_second], axis=0)
        own = part[6 * half :].astype(jnp.float32)
        own = own + arrived_left.astype(jnp.float32) + arrived_right.astype(jnp.float32)
        back = exchange(own.astype(jnp.bfloat16).reshape(experts, capacity, width))
        back = back.reshape(slots, width)
        mixed = jnp.dot(mix_high, back, preferred_element_type=jnp.float32)
        mixed = mixed + jnp.dot(mix_low, back, preferred_element_type=jnp.float32)
        results.append((widened[:, cols] + mixed).astype(jnp.bfloat16))
    return jnp.concatenate(results, axis=1)[None]


def solution(mesh):
    placed = (
        P("section", "expert", None),
        P("section", None),
        P("section", "expert", None),
        P("section", "expert", None),
        P("section", None, "expert"),
        P("section", None, "expert"),
        P("section", "expert", None),
    )
    return jax.shard_map(
        body, mesh=mesh, in_specs=placed, out_specs=P("section", "expert", None), check_vma=False
    )
```

```python
import functools

import jax
import jax.numpy as jnp
from jax import lax
from jax.experimental import pallas as pl
from jax.experimental.pallas import tpu as pltpu
from jax.sharding import PartitionSpec as P

FF_WIN = 1024
HID_DEV = 256
CHUNKS = 2
PAD = 8

epsilon = 1e-06


def gate_up_kernel(pieces, steps, last, *refs):
    piece_refs = refs[:pieces]
    gate_ref, up_ref = refs[pieces : pieces + 2]
    rest = refs[pieces + 2 :]
    start_refs, out_ref, acc_ref = rest[:-2], rest[-2], rest[-1]
    step = pl.program_id(0)

    @pl.when(step == 0)
    def _():
        if start_refs:
            acc_ref[...] = start_refs[0][...]
        else:
            acc_ref[...] = jnp.zeros_like(acc_ref)

    rows = jnp.concatenate([ref[...] for ref in piece_refs], axis=0)
    hid = gate_ref.shape[1]
    acc_ref[:, :hid] += jnp.dot(rows, gate_ref[...], preferred_element_type=jnp.float32)
    acc_ref[:, hid:] += jnp.dot(rows, up_ref[...], preferred_element_type=jnp.float32)

    @pl.when(step == steps - 1)
    def _():
        if last:
            gate = acc_ref[:, :hid]
            out_ref[...] = (gate / (1.0 + jnp.exp(-gate)) * acc_ref[:, hid:]).astype(out_ref.dtype)
        else:
            out_ref[...] = acc_ref[...]


def gate_up(pieces, gate_weight, up_weight, first_row, before, last):
    piece_rows, width = pieces[0].shape
    depth = 512
    steps = width // depth
    offset = first_row // depth
    rows = piece_rows * len(pieces)
    hid = gate_weight.shape[1]
    start = [] if before is None else [before]
    out_shape = (rows, hid) if last else (rows, 2 * hid)
    out_type = jnp.bfloat16 if last else jnp.float32
    return pl.pallas_call(
        functools.partial(gate_up_kernel, len(pieces), steps, last),
        grid=(steps,),
        in_specs=[pl.BlockSpec((piece_rows, depth), lambda k: (0, k)) for _ in pieces]
        + [pl.BlockSpec((depth, hid), lambda k: (k + offset, 0))] * 2
        + [pl.BlockSpec((rows, 2 * hid), lambda k: (0, 0)) for _ in start],
        out_specs=pl.BlockSpec(out_shape, lambda k: (0, 0)),
        out_shape=jax.ShapeDtypeStruct(out_shape, out_type),
        scratch_shapes=[pltpu.VMEM((rows, 2 * hid), jnp.float32)],
        compiler_params=pltpu.CompilerParams(vmem_limit_bytes=40 << 20),
        cost_estimate=pl.CostEstimate(
            flops=4 * rows * hid * width, bytes_accessed=2 * (rows + 2 * hid) * width, transcendentals=0
        ),
        name="gate_up",
    )(*pieces, gate_weight, up_weight, *start)


def down_kernel(orders, *refs):
    parts = len(orders)
    hid_refs, weight_refs = refs[:parts], refs[parts : 2 * parts]
    spread_ref, out_ref, spread_hid = refs[2 * parts :]
    hid = hid_refs[0].shape[1]
    block = hid_refs[0].shape[0] // parts

    @pl.when(pl.program_id(0) == 0)
    def _():
        for j in range(parts):
            rows = jnp.concatenate(
                [hid_refs[j][b * block : (b + 1) * block, :] for b in orders[j]], axis=0
            )
            spread_hid[:, j * hid : (j + 1) * hid] = jnp.dot(
                spread_ref[...], rows, preferred_element_type=jnp.float32
            ).astype(spread_hid.dtype)

    weights = jnp.concatenate([ref[...] for ref in weight_refs], axis=0)
    out_ref[...] = jnp.dot(spread_hid[...], weights, preferred_element_type=jnp.float32).astype(
        out_ref.dtype
    )


def down(hiddens, weights, spread, orders):
    rows, hid = hiddens[0].shape
    out_rows, width = spread.shape[0], weights[0].shape[1]
    cols = 896
    parts = len(orders)
    return pl.pallas_call(
        functools.partial(down_kernel, orders),
        grid=(width // cols,),
        in_specs=[pl.BlockSpec((rows, hid), lambda n: (0, 0))] * parts
        + [pl.BlockSpec((hid, cols), lambda n: (0, n))] * parts
        + [pl.BlockSpec(spread.shape, lambda n: (0, 0))],
        out_specs=pl.BlockSpec((out_rows, cols), lambda n: (0, n)),
        out_shape=jax.ShapeDtypeStruct((out_rows, width), jnp.bfloat16),
        scratch_shapes=[pltpu.VMEM((out_rows, parts * hid), jnp.bfloat16)],
        compiler_params=pltpu.CompilerParams(vmem_limit_bytes=40 << 20),
        cost_estimate=pl.CostEstimate(
            flops=2 * out_rows * parts * hid * (width + rows),
            bytes_accessed=2 * (out_rows + parts * hid) * width,
            transcendentals=0,
        ),
        name="down",
    )(*hiddens, *weights, spread)


def mix_kernel(parts, width, returned_ref, mixing_ref, inbound_ref, out_ref):
    tokens = inbound_ref.shape[0]
    cols = returned_ref.shape[1]
    start = pl.program_id(0) * cols
    product = jnp.dot(mixing_ref[...], returned_ref[...], preferred_element_type=jnp.float32)
    for f in range(parts):
        at = pl.ds(pl.multiple_of(f * width + start, 128), cols)
        high = product[f * tokens : (f + 1) * tokens]
        low = product[(parts + f) * tokens : (parts + f + 1) * tokens]
        total = inbound_ref[:, at].astype(jnp.float32) + (high + low)
        out_ref[:, at] = total.astype(out_ref.dtype)


def mix(returned, mixing, inbound, parts):
    rows, width = returned.shape
    cols = 256
    return pl.pallas_call(
        functools.partial(mix_kernel, parts, width),
        grid=(width // cols,),
        in_specs=[
            pl.BlockSpec((rows, cols), lambda n: (0, n)),
            pl.BlockSpec(mixing.shape, lambda n: (0, 0)),
            pl.BlockSpec(inbound.shape, lambda n: (0, 0)),
        ],
        out_specs=pl.BlockSpec(inbound.shape, lambda n: (0, 0)),
        out_shape=jax.ShapeDtypeStruct(inbound.shape, inbound.dtype),
        compiler_params=pltpu.CompilerParams(vmem_limit_bytes=40 << 20),
        name="mix",
    )(returned, mixing, inbound)


def body(arriving, gains, routes, combine_weight, gate_weight, up_weight, down_weight):
    device_count = lax.axis_size("expert")
    ring = FF_WIN // HID_DEV
    experts = device_count // ring
    tok_count = arriving.shape[1]
    feature_count = arriving.shape[2]
    top_count = routes.shape[2]
    capacity = min(tok_count, 5 * tok_count * top_count // (4 * experts))
    slots = experts * capacity
    padded = experts * PAD
    half = slots // 2
    width = feature_count // CHUNKS
    quarter = feature_count // ring
    planes = [[g * ring + r for g in range(experts)] for r in range(ring)]
    place = lax.rem(lax.axis_index("expert"), ring)

    def shift(block, step):
        route = [(i, i - i % ring + (i + step) % ring) for i in range(device_count)]
        return lax.ppermute(block, "expert", route)

    def exchange(block, groups):
        return lax.all_to_all(
            block, "expert", split_axis=0, concat_axis=0, axis_index_groups=groups, tiled=True
        )

    def weight_part(step):
        start = lax.rem(place + step, ring) * quarter
        return lax.dynamic_slice_in_dim(down_weight[0], start, quarter, 1)

    other = [(i, 1 - i) for i in range(2)]
    inbound = lax.ppermute(arriving, "section", other)[0]
    down_parts = [
        weight_part(0),
        shift(weight_part(1), 1),
        shift(weight_part(3), -1),
        shift(weight_part(2), 2),
    ]
    widened = inbound.astype(jnp.float32)
    inv_rms = lax.rsqrt(jnp.mean(widened * widened, axis=-1, keepdims=True) + epsilon)
    normed = (widened * inv_rms * gains[0][None, :]).astype(jnp.bfloat16)
    chosen = routes[0].reshape(-1)
    onehot = (chosen[:, None] == jnp.arange(experts, dtype=jnp.int32)[None, :]).astype(jnp.int32)
    earlier = jnp.cumsum(onehot, axis=0) - onehot
    slot_index = jnp.sum(earlier * onehot, axis=1)
    target = (chosen * PAD + slot_index).reshape(tok_count, top_count)
    slot_ids = jnp.arange(padded, dtype=jnp.int32)
    hits = target[:, :, None] == slot_ids[None, None, :]
    placement = jnp.any(hits, axis=1).astype(jnp.bfloat16).T

    def rows_of(count, size):
        ids = jnp.arange(count * size, dtype=jnp.int32)
        return ids // size, ids % size

    to_block, to_slot = rows_of(experts // 2, capacity)
    from_block, from_slot = rows_of(experts // 2, PAD)
    squeeze = (to_block * PAD + to_slot)[:, None] == (from_block * PAD + from_slot)[None, :]
    squeeze = squeeze.astype(jnp.bfloat16)

    def squeezed(block):
        return jnp.dot(squeeze, block, preferred_element_type=jnp.float32).astype(jnp.bfloat16)

    packed = [
        jnp.dot(placement, normed[:, c * width : (c + 1) * width], preferred_element_type=jnp.float32)
        .astype(jnp.bfloat16)
        .reshape(experts, PAD, width)
        for c in range(CHUNKS)
    ]
    state = None
    for c in range(CHUNKS):
        landed = exchange(packed[c], planes).reshape(padded, width)
        if c == 0:
            landed, *down_parts = lax.optimization_barrier((landed, *down_parts))
        first, second = squeezed(landed[: padded // 2]), squeezed(landed[padded // 2 :])
        if c + 1 < CHUNKS:
            first, second, packed[c + 1] = lax.optimization_barrier((first, second, packed[c + 1]))
        left_first, right_second = shift(first, 1), shift(second, -1)
        left_second, right_first = shift(second, 1), shift(first, -1)
        far_first, far_second = shift(left_first, 1), shift(right_second, -1)
        pieces = [
            first, second, left_first, left_second, right_first, right_second, far_first, far_second
        ]
        state = gate_up(
            pieces, gate_weight[0], up_weight[0], c * width, state, c == CHUNKS - 1
        )
    hiddens = [state, shift(state, 1), shift(state, -1), shift(state, 2)]
    orders = ((0, 1, 2, 3), (2, 0, 3, 1), (1, 3, 0, 2), (3, 2, 1, 0))

    row = jnp.arange(device_count * PAD, dtype=jnp.int32)
    column = jnp.arange(ring * slots, dtype=jnp.int32)
    relative = column // slots
    away = jnp.where(relative == 1, ring - 1, jnp.where(relative == 2, 1, jnp.where(relative == 3, 2, 0)))
    origin = lax.rem(place + away, jnp.int32(ring))
    inner = column % slots
    goal = (inner // capacity * ring + origin) * PAD + inner % capacity
    spread = (row[:, None] == goal[None, :]).astype(jnp.bfloat16)
    complete = down(hiddens, down_parts, spread, orders)
    returned = exchange(complete.reshape(device_count, PAD, quarter), None)
    returned = returned.reshape(device_count * PAD, quarter)

    mixing = jnp.sum(jnp.where(hits, combine_weight[0][:, :, None], 0.0), axis=1)
    mix_high = lax.reduce_precision(mixing, 8, 7)
    both = jnp.stack([mix_high, mixing - mix_high]).astype(jnp.bfloat16)
    both = both.reshape(2, 1, tok_count, experts, 1, PAD)
    same = jnp.arange(ring)[:, None] == jnp.arange(ring)[None, :]
    both = jnp.where(same[None, :, None, None, :, None], both, jnp.bfloat16(0))
    both = both.reshape(2 * ring * tok_count, device_count * PAD)
    return mix(returned, both, inbound, ring)[None]


def solution(mesh):
    placed = (
        P("section", "expert", None),
        P("section", None),
        P("section", "expert", None),
        P("section", "expert", None),
        P("section", None, "expert"),
        P("section", None, "expert"),
        P("section", "expert", None),
    )
    return jax.shard_map(
        body, mesh=mesh, in_specs=placed, out_specs=P("section", "expert", None), check_vma=False
    )
```

```python
import functools

import jax
import jax.numpy as jnp
from jax import lax
from jax.experimental import pallas as pl
from jax.experimental.pallas import tpu as pltpu
from jax.sharding import PartitionSpec as P

FF_WIN = 1024
HID_DEV = 256
WIDTHS = (4096, 3072)
FOLD = 8
PAD = 8
VMEM = 40 << 20

epsilon = 1e-06


def unfold_kernel(sort_ref, landed_ref, *out_refs):
    cols = landed_ref.shape[1]
    rows = landed_ref.shape[0] // len(out_refs)
    for h, out_ref in enumerate(out_refs):
        count = out_ref.shape[0]
        part = landed_ref[h * rows : (h + 1) * rows, :]
        sorted_part = jnp.dot(sort_ref[...], part, preferred_element_type=jnp.float32)
        sorted_part = sorted_part.astype(out_ref.dtype)
        for f in range(FOLD):
            out_ref[:, f * cols : (f + 1) * cols] = sorted_part[f * count : (f + 1) * count]


def unfold(landed, sort):
    rows, cols = landed.shape
    count = sort.shape[0] // FOLD
    halves = rows // sort.shape[0]
    shape = jax.ShapeDtypeStruct((count, cols * FOLD), landed.dtype)
    return pl.pallas_call(
        unfold_kernel,
        out_shape=[shape] * halves,
        compiler_params=pltpu.CompilerParams(vmem_limit_bytes=VMEM),
        name="unfold",
    )(sort, landed)


def gate_up_kernel(pieces, steps, last, *refs):
    piece_refs = refs[:pieces]
    gate_ref, up_ref = refs[pieces : pieces + 2]
    rest = refs[pieces + 2 :]
    start_refs, out_ref, acc_ref = rest[:-2], rest[-2], rest[-1]
    step = pl.program_id(0)

    @pl.when(step == 0)
    def _():
        if start_refs:
            acc_ref[...] = start_refs[0][...]
        else:
            acc_ref[...] = jnp.zeros_like(acc_ref)

    rows = jnp.concatenate([ref[...] for ref in piece_refs], axis=0)
    hid = gate_ref.shape[1]
    acc_ref[:, :hid] += jnp.dot(rows, gate_ref[...], preferred_element_type=jnp.float32)
    acc_ref[:, hid:] += jnp.dot(rows, up_ref[...], preferred_element_type=jnp.float32)

    @pl.when(step == steps - 1)
    def _():
        if last:
            gate = acc_ref[:, :hid]
            out_ref[...] = (gate / (1.0 + jnp.exp(-gate)) * acc_ref[:, hid:]).astype(out_ref.dtype)
        else:
            out_ref[...] = acc_ref[...]


def gate_up(pieces, gate_weight, up_weight, first_row, before, block, last):
    piece_rows, width = pieces[0].shape
    depth = 1024
    steps = width // depth
    offset = first_row // depth
    rows = piece_rows * len(pieces)
    hid = gate_weight.shape[1]
    start = [] if before is None else [before]
    out_shape = (rows, hid) if last else (rows, 2 * hid)
    out_type = jnp.bfloat16 if last else jnp.float32
    return pl.pallas_call(
        functools.partial(gate_up_kernel, len(pieces), steps, last),
        grid=(steps,),
        in_specs=[pl.BlockSpec((piece_rows, depth), lambda k: (0, k)) for _ in pieces]
        + [pl.BlockSpec((depth, hid), lambda k: (k + offset, 0))] * 2
        + [pl.BlockSpec((rows, 2 * hid), lambda k: (block, 0)) for _ in start],
        out_specs=pl.BlockSpec(out_shape, lambda k: (0, 0)),
        out_shape=jax.ShapeDtypeStruct(out_shape, out_type),
        scratch_shapes=[pltpu.VMEM((rows, 2 * hid), jnp.float32)],
        compiler_params=pltpu.CompilerParams(vmem_limit_bytes=VMEM),
        cost_estimate=pl.CostEstimate(
            flops=4 * rows * hid * width, bytes_accessed=2 * (rows + 2 * hid) * width, transcendentals=0
        ),
        name="gate_up",
    )(*pieces, gate_weight, up_weight, *start)


def down_kernel(orders, *refs):
    parts = len(orders)
    near_refs, far_refs = refs[:parts], refs[parts : 2 * parts]
    weight_refs = refs[2 * parts : 3 * parts]
    spread_ref, out_ref, spread_hid = refs[3 * parts :]
    block, hid = far_refs[0].shape

    @pl.when(pl.program_id(0) == 0)
    def _():
        for j in range(parts):
            blocks = [near_refs[j][b * block : (b + 1) * block, :] for b in range(parts - 1)]
            blocks.append(far_refs[j][...])
            rows = jnp.concatenate([blocks[b] for b in orders[j]], axis=0)
            spread_hid[:, j * hid : (j + 1) * hid] = jnp.dot(
                spread_ref[...], rows, preferred_element_type=jnp.float32
            ).astype(spread_hid.dtype)

    weights = jnp.concatenate([ref[...] for ref in weight_refs], axis=0)
    out_ref[...] = jnp.dot(spread_hid[...], weights, preferred_element_type=jnp.float32).astype(
        out_ref.dtype
    )


def down(near, far, weights, spread, orders):
    hid = far[0].shape[1]
    out_rows, width = spread.shape[0], weights[0].shape[1]
    cols = width // 2
    parts = len(orders)
    return pl.pallas_call(
        functools.partial(down_kernel, orders),
        grid=(width // cols,),
        in_specs=[pl.BlockSpec(near[0].shape, lambda n: (0, 0))] * parts
        + [pl.BlockSpec(far[0].shape, lambda n: (0, 0))] * parts
        + [pl.BlockSpec((hid, cols), lambda n: (0, n))] * parts
        + [pl.BlockSpec(spread.shape, lambda n: (0, 0))],
        out_specs=pl.BlockSpec((out_rows, cols), lambda n: (0, n)),
        out_shape=jax.ShapeDtypeStruct((out_rows, width), jnp.bfloat16),
        scratch_shapes=[pltpu.VMEM((out_rows, parts * hid), jnp.bfloat16)],
        compiler_params=pltpu.CompilerParams(vmem_limit_bytes=VMEM),
        cost_estimate=pl.CostEstimate(
            flops=2 * out_rows * parts * hid * (width + spread.shape[1]),
            bytes_accessed=2 * (out_rows + parts * hid) * width,
            transcendentals=0,
        ),
        name="down",
    )(*near, *far, *weights, spread)


def mix_kernel(parts, width, returned_ref, mixing_ref, inbound_ref, out_ref):
    tokens = inbound_ref.shape[0]
    cols = returned_ref.shape[1]
    start = pl.program_id(0) * cols
    product = jnp.dot(mixing_ref[...], returned_ref[...], preferred_element_type=jnp.float32)
    for f in range(parts):
        at = pl.ds(pl.multiple_of(f * width + start, 128), cols)
        high = product[f * tokens : (f + 1) * tokens]
        low = product[(parts + f) * tokens : (parts + f + 1) * tokens]
        total = inbound_ref[:, at].astype(jnp.float32) + (high + low)
        out_ref[:, at] = total.astype(out_ref.dtype)


def mix(returned, mixing, inbound, parts):
    rows, width = returned.shape
    cols = 896
    return pl.pallas_call(
        functools.partial(mix_kernel, parts, width),
        grid=(width // cols,),
        in_specs=[
            pl.BlockSpec((rows, cols), lambda n: (0, n)),
            pl.BlockSpec(mixing.shape, lambda n: (0, 0)),
            pl.BlockSpec(inbound.shape, lambda n: (0, 0)),
        ],
        out_specs=pl.BlockSpec(inbound.shape, lambda n: (0, 0)),
        out_shape=jax.ShapeDtypeStruct(inbound.shape, inbound.dtype),
        compiler_params=pltpu.CompilerParams(vmem_limit_bytes=VMEM),
        name="mix",
    )(returned, mixing, inbound)


def body(arriving, gains, routes, combine_weight, gate_weight, up_weight, down_weight):
    device_count = lax.axis_size("expert")
    ring = FF_WIN // HID_DEV
    experts = device_count // ring
    tok_count = arriving.shape[1]
    feature_count = arriving.shape[2]
    top_count = routes.shape[2]
    capacity = min(tok_count, 5 * tok_count * top_count // (4 * experts))
    slots = experts * capacity
    half = slots // 2
    quarter = feature_count // ring
    planes = [[g * ring + r for g in range(experts)] for r in range(ring)]
    place = lax.rem(lax.axis_index("expert"), ring)

    def shift(block, step):
        route = [(i, i - i % ring + (i + step) % ring) for i in range(device_count)]
        return lax.ppermute(block, "expert", route)

    def exchange(block, groups):
        return lax.all_to_all(
            block, "expert", split_axis=0, concat_axis=0, axis_index_groups=groups, tiled=True
        )

    def weight_part(step):
        start = lax.rem(place + step, ring) * quarter
        return lax.dynamic_slice_in_dim(down_weight[0], start, quarter, 1)

    def numbers(count):
        return jnp.arange(count, dtype=jnp.int32)

    other = [(i, 1 - i) for i in range(2)]
    inbound = lax.ppermute(arriving, "section", other)[0]
    down_parts = [
        weight_part(0),
        shift(weight_part(1), 1),
        shift(weight_part(3), -1),
        shift(weight_part(2), 2),
    ]
    widened = inbound.astype(jnp.float32)
    inv_rms = lax.rsqrt(jnp.mean(widened * widened, axis=-1, keepdims=True) + epsilon)
    normed = (widened * inv_rms * gains[0][None, :]).astype(jnp.bfloat16)
    chosen = routes[0].reshape(-1)
    onehot = (chosen[:, None] == jnp.arange(experts, dtype=jnp.int32)[None, :]).astype(jnp.int32)
    earlier = jnp.cumsum(onehot, axis=0) - onehot
    slot_index = jnp.sum(earlier * onehot, axis=1)
    target = (chosen * PAD + slot_index).reshape(tok_count, top_count)

    row, token = numbers(experts * FOLD * capacity), numbers(FOLD * tok_count)
    code = row // (FOLD * capacity) * PAD + row % capacity
    hits = jnp.any(jnp.tile(target, (FOLD, 1))[None, :, :] == code[:, None, None], axis=2)
    hits = hits & ((row % (FOLD * capacity) // capacity)[:, None] == (token // tok_count)[None, :])
    placement = hits.astype(jnp.bfloat16)
    packed, firsts = [], []
    for width in WIDTHS:
        firsts.append(firsts[-1] + WIDTHS[len(firsts) - 1] if firsts else 0)
        cols = width // FOLD
        cuts = [firsts[-1] + f * cols for f in range(FOLD)]
        folded = jnp.concatenate([normed[:, cut : cut + cols] for cut in cuts], axis=0)
        block = jnp.dot(placement, folded, preferred_element_type=jnp.float32)
        packed.append(block.astype(jnp.bfloat16).reshape(experts, FOLD * capacity, cols))

    to_row, from_row = numbers(FOLD * half), numbers(FOLD * half)
    wanted = to_row % half // capacity * (FOLD * capacity) + to_row // half * capacity + to_row % capacity
    sort = (wanted[:, None] == from_row[None, :]).astype(jnp.bfloat16)

    gate, up = gate_weight[0], up_weight[0]
    packed[1], *down_parts = lax.optimization_barrier((packed[1], *down_parts))
    landed = [exchange(block, planes) for block in packed]
    landed = [block.reshape(FOLD * slots, block.shape[2]) for block in landed]
    arrived = []
    for c in range(len(WIDTHS)):
        if c > 0:
            early = arrived[c - 1][2], arrived[c - 1][5]
            landed[c] = lax.optimization_barrier((landed[c], *early))[0]
        first, second = unfold(landed[c], sort)
        left_first, right_second = shift(first, 1), shift(second, -1)
        left_second, right_first = shift(second, 1), shift(first, -1)
        far_first, far_second = shift(left_first, 1), shift(right_second, -1)
        arrived.append(
            [first, second, left_first, left_second, right_first, right_second, far_first, far_second]
        )
    state = None
    for c in range(len(WIDTHS) - 1):
        early = arrived[c + 1][2], arrived[c + 1][5]
        begun = list(lax.optimization_barrier((*arrived[c], *early))[: len(arrived[c])])
        state = gate_up(begun, gate, up, firsts[c], state, 0, False)
    mine_near = gate_up(arrived[-1][:6], gate, up, firsts[-1], state, 0, True)
    near = [mine_near, shift(mine_near, 1), shift(mine_near, -1), shift(mine_near, 2)]
    mine_far = gate_up(arrived[-1][6:], gate, up, firsts[-1], state, 3, True)
    far = [mine_far, shift(mine_far, 1), shift(mine_far, -1), shift(mine_far, 2)]
    orders = ((0, 1, 2, 3), (2, 0, 3, 1), (1, 3, 0, 2), (3, 2, 1, 0))

    row = jnp.arange(device_count * PAD, dtype=jnp.int32)
    column = jnp.arange(ring * slots, dtype=jnp.int32)
    relative = column // slots
    away = jnp.where(relative == 1, ring - 1, jnp.where(relative == 2, 1, jnp.where(relative == 3, 2, 0)))
    origin = lax.rem(place + away, jnp.int32(ring))
    inner = column % slots
    goal = (inner // capacity * ring + origin) * PAD + inner % capacity
    spread = (row[:, None] == goal[None, :]).astype(jnp.bfloat16)
    complete = down(near, far, down_parts, spread, orders)
    returned = exchange(complete.reshape(device_count, PAD, quarter), None)
    returned = returned.reshape(device_count * PAD, quarter)

    hits = target[:, :, None] == numbers(experts * PAD)[None, None, :]
    mixing = jnp.sum(jnp.where(hits, combine_weight[0][:, :, None], 0.0), axis=1)
    mix_high = lax.reduce_precision(mixing, 8, 7)
    both = jnp.stack([mix_high, mixing - mix_high]).astype(jnp.bfloat16)
    both = both.reshape(2, 1, tok_count, experts, 1, PAD)
    same = jnp.arange(ring)[:, None] == jnp.arange(ring)[None, :]
    both = jnp.where(same[None, :, None, None, :, None], both, jnp.bfloat16(0))
    both = both.reshape(2 * ring * tok_count, device_count * PAD)
    return mix(returned, both, inbound, ring)[None]


def solution(mesh):
    placed = (
        P("section", "expert", None),
        P("section", None),
        P("section", "expert", None),
        P("section", "expert", None),
        P("section", None, "expert"),
        P("section", None, "expert"),
        P("section", "expert", None),
    )
    return jax.shard_map(
        body, mesh=mesh, in_specs=placed, out_specs=P("section", "expert", None), check_vma=False
    )
```

```python
import functools

import jax
import jax.numpy as jnp
from jax import lax
from jax.experimental import pallas as pl
from jax.experimental.pallas import tpu as pltpu
from jax.sharding import PartitionSpec as P

FF_WIN = 1024
HID_DEV = 256
WIDTHS = (4096, 3072)
FOLD = 8
PAD = 8
VMEM = 40 << 20

epsilon = 1e-06


def unfold_kernel(parts, sort_ref, landed_ref, *out_refs):
    cols = landed_ref.shape[1]
    rows = sort_ref.shape[0]
    count = out_refs[0].shape[0]
    halves = len(out_refs) // parts
    for h in range(halves):
        part = landed_ref[h * rows : (h + 1) * rows, :]
        sorted_part = jnp.dot(sort_ref[...], part, preferred_element_type=jnp.float32)
        sorted_part = sorted_part.astype(landed_ref.dtype)
        for q in range(rows // count):
            fold, part_index = q // parts, q % parts
            out_ref = out_refs[part_index * halves + h]
            out_ref[:, fold * cols : (fold + 1) * cols] = sorted_part[q * count : (q + 1) * count]


def unfold(landed, sort, count, parts):
    rows, cols = landed.shape
    halves = rows // sort.shape[0]
    folds = sort.shape[0] // count // parts
    shape = jax.ShapeDtypeStruct((count, cols * folds), landed.dtype)
    return pl.pallas_call(
        functools.partial(unfold_kernel, parts),
        out_shape=[shape] * (halves * parts),
        compiler_params=pltpu.CompilerParams(vmem_limit_bytes=VMEM),
        cost_estimate=pl.CostEstimate(
            flops=2 * rows * cols * sort.shape[0], bytes_accessed=4 * landed.size, transcendentals=0
        ),
        name="unfold",
    )(sort, landed)


def gate_up_kernel(pieces, steps, last, *refs):
    piece_refs = refs[:pieces]
    gate_ref, up_ref = refs[pieces : pieces + 2]
    rest = refs[pieces + 2 :]
    start_refs, out_ref, acc_ref = rest[:-2], rest[-2], rest[-1]
    step = pl.program_id(0)

    @pl.when(step == 0)
    def _():
        if start_refs:
            acc_ref[...] = start_refs[0][...]
        else:
            acc_ref[...] = jnp.zeros_like(acc_ref)

    rows = jnp.concatenate([ref[...] for ref in piece_refs], axis=0)
    hid = gate_ref.shape[1]
    acc_ref[:, :hid] += jnp.dot(rows, gate_ref[...], preferred_element_type=jnp.float32)
    acc_ref[:, hid:] += jnp.dot(rows, up_ref[...], preferred_element_type=jnp.float32)

    @pl.when(step == steps - 1)
    def _():
        if last:
            gate = acc_ref[:, :hid]
            out_ref[...] = (gate / (1.0 + jnp.exp(-gate)) * acc_ref[:, hid:]).astype(out_ref.dtype)
        else:
            out_ref[...] = acc_ref[...]


def gate_up(pieces, gate_weight, up_weight, first_row, before, block, last):
    piece_rows, width = pieces[0].shape
    depth = 1024
    steps = width // depth
    offset = first_row // depth
    rows = piece_rows * len(pieces)
    hid = gate_weight.shape[1]
    start = [] if before is None else [before]
    out_shape = (rows, hid) if last else (rows, 2 * hid)
    out_type = jnp.bfloat16 if last else jnp.float32
    return pl.pallas_call(
        functools.partial(gate_up_kernel, len(pieces), steps, last),
        grid=(steps,),
        in_specs=[pl.BlockSpec((piece_rows, depth), lambda k: (0, k)) for _ in pieces]
        + [pl.BlockSpec((depth, hid), lambda k: (k + offset, 0))] * 2
        + [pl.BlockSpec((rows, 2 * hid), lambda k: (block, 0)) for _ in start],
        out_specs=pl.BlockSpec(out_shape, lambda k: (0, 0)),
        out_shape=jax.ShapeDtypeStruct(out_shape, out_type),
        scratch_shapes=[pltpu.VMEM((rows, 2 * hid), jnp.float32)],
        compiler_params=pltpu.CompilerParams(vmem_limit_bytes=VMEM),
        cost_estimate=pl.CostEstimate(
            flops=4 * rows * hid * width, bytes_accessed=2 * (rows + 2 * hid) * width, transcendentals=0
        ),
        name="gate_up",
    )(*pieces, gate_weight, up_weight, *start)


def down_kernel(orders, *refs):
    parts = len(orders)
    near_refs, far_refs = refs[:parts], refs[parts : 2 * parts]
    weight_refs = refs[2 * parts : 3 * parts]
    spread_ref, out_ref, spread_hid = refs[3 * parts :]
    block, hid = far_refs[0].shape

    @pl.when(pl.program_id(0) == 0)
    def _():
        for j in range(parts):
            blocks = [near_refs[j][b * block : (b + 1) * block, :] for b in range(parts - 1)]
            blocks.append(far_refs[j][...])
            rows = jnp.concatenate([blocks[b] for b in orders[j]], axis=0)
            spread_hid[:, j * hid : (j + 1) * hid] = jnp.dot(
                spread_ref[...], rows, preferred_element_type=jnp.float32
            ).astype(spread_hid.dtype)

    weights = jnp.concatenate([ref[...] for ref in weight_refs], axis=0)
    out_ref[...] = jnp.dot(spread_hid[...], weights, preferred_element_type=jnp.float32).astype(
        out_ref.dtype
    )


def down(near, far, weights, spread, orders):
    hid = far[0].shape[1]
    out_rows, width = spread.shape[0], weights[0].shape[1]
    cols = width // 2
    parts = len(orders)
    return pl.pallas_call(
        functools.partial(down_kernel, orders),
        grid=(width // cols,),
        in_specs=[pl.BlockSpec(near[0].shape, lambda n: (0, 0))] * parts
        + [pl.BlockSpec(far[0].shape, lambda n: (0, 0))] * parts
        + [pl.BlockSpec((hid, cols), lambda n: (0, n))] * parts
        + [pl.BlockSpec(spread.shape, lambda n: (0, 0))],
        out_specs=pl.BlockSpec((out_rows, cols), lambda n: (0, n)),
        out_shape=jax.ShapeDtypeStruct((out_rows, width), jnp.bfloat16),
        scratch_shapes=[pltpu.VMEM((out_rows, parts * hid), jnp.bfloat16)],
        compiler_params=pltpu.CompilerParams(vmem_limit_bytes=VMEM),
        cost_estimate=pl.CostEstimate(
            flops=2 * out_rows * parts * hid * (width + spread.shape[1]),
            bytes_accessed=2 * (out_rows + parts * hid) * width,
            transcendentals=0,
        ),
        name="down",
    )(*near, *far, *weights, spread)


def mix_kernel(parts, width, returned_ref, mixing_ref, inbound_ref, out_ref):
    tokens = inbound_ref.shape[0]
    cols = returned_ref.shape[1]
    start = pl.program_id(0) * cols
    product = jnp.dot(mixing_ref[...], returned_ref[...], preferred_element_type=jnp.float32)
    for f in range(parts):
        at = pl.ds(pl.multiple_of(f * width + start, 128), cols)
        high = product[f * tokens : (f + 1) * tokens]
        low = product[(parts + f) * tokens : (parts + f + 1) * tokens]
        total = inbound_ref[:, at].astype(jnp.float32) + (high + low)
        out_ref[:, at] = total.astype(out_ref.dtype)


def mix(returned, mixing, inbound, parts):
    rows, width = returned.shape
    cols = 896
    return pl.pallas_call(
        functools.partial(mix_kernel, parts, width),
        grid=(width // cols,),
        in_specs=[
            pl.BlockSpec((rows, cols), lambda n: (0, n)),
            pl.BlockSpec(mixing.shape, lambda n: (0, 0)),
            pl.BlockSpec(inbound.shape, lambda n: (0, 0)),
        ],
        out_specs=pl.BlockSpec(inbound.shape, lambda n: (0, 0)),
        out_shape=jax.ShapeDtypeStruct(inbound.shape, inbound.dtype),
        compiler_params=pltpu.CompilerParams(vmem_limit_bytes=VMEM),
        name="mix",
    )(returned, mixing, inbound)


def body(arriving, gains, routes, combine_weight, gate_weight, up_weight, down_weight):
    device_count = lax.axis_size("expert")
    ring = FF_WIN // HID_DEV
    experts = device_count // ring
    tok_count = arriving.shape[1]
    feature_count = arriving.shape[2]
    top_count = routes.shape[2]
    capacity = min(tok_count, 5 * tok_count * top_count // (4 * experts))
    slots = experts * capacity
    half = slots // 2
    quarter = feature_count // ring
    planes = [[g * ring + r for g in range(experts)] for r in range(ring)]
    place = lax.rem(lax.axis_index("expert"), ring)

    def shift(block, step):
        route = [(i, i - i % ring + (i + step) % ring) for i in range(device_count)]
        return lax.ppermute(block, "expert", route)

    def exchange(block, groups):
        return lax.all_to_all(
            block, "expert", split_axis=0, concat_axis=0, axis_index_groups=groups, tiled=True
        )

    def weight_part(step):
        start = lax.rem(place + step, ring) * quarter
        return lax.dynamic_slice_in_dim(down_weight[0], start, quarter, 1)

    def numbers(count):
        return jnp.arange(count, dtype=jnp.int32)

    other = [(i, 1 - i) for i in range(2)]
    inbound = lax.ppermute(arriving, "section", other)[0]
    down_parts = [
        weight_part(0),
        shift(weight_part(1), 1),
        shift(weight_part(3), -1),
        shift(weight_part(2), 2),
    ]
    widened = inbound.astype(jnp.float32)
    inv_rms = lax.rsqrt(jnp.mean(widened * widened, axis=-1, keepdims=True) + epsilon)
    normed = (widened * inv_rms * gains[0][None, :]).astype(jnp.bfloat16)
    chosen = routes[0].reshape(-1)
    onehot = (chosen[:, None] == jnp.arange(experts, dtype=jnp.int32)[None, :]).astype(jnp.int32)
    earlier = jnp.cumsum(onehot, axis=0) - onehot
    slot_index = jnp.sum(earlier * onehot, axis=1)
    target = (chosen * PAD + slot_index).reshape(tok_count, top_count)

    row, token = numbers(experts * FOLD * capacity), numbers(FOLD * tok_count)
    code = row // (FOLD * capacity) * PAD + row % capacity
    hits = jnp.any(jnp.tile(target, (FOLD, 1))[None, :, :] == code[:, None, None], axis=2)
    hits = hits & ((row % (FOLD * capacity) // capacity)[:, None] == (token // tok_count)[None, :])
    placement = hits.astype(jnp.bfloat16)
    packed, firsts = [], []
    for width in WIDTHS:
        firsts.append(firsts[-1] + WIDTHS[len(firsts) - 1] if firsts else 0)
        cols = width // FOLD
        cuts = [firsts[-1] + f * cols for f in range(FOLD)]
        folded = jnp.concatenate([normed[:, cut : cut + cols] for cut in cuts], axis=0)
        block = jnp.dot(placement, folded, preferred_element_type=jnp.float32)
        packed.append(block.astype(jnp.bfloat16).reshape(experts, FOLD * capacity, cols))

    to_row, from_row = numbers(FOLD * half), numbers(FOLD * half)
    wanted = to_row % half // capacity * (FOLD * capacity) + to_row // half * capacity + to_row % capacity
    sort = (wanted[:, None] == from_row[None, :]).astype(jnp.bfloat16)

    gate, up = gate_weight[0], up_weight[0]
    packed[1], *down_parts = lax.optimization_barrier((packed[1], *down_parts))
    landed = [exchange(block, planes) for block in packed]
    landed = [block.reshape(FOLD * slots, block.shape[2]) for block in landed]
    arrived = []
    for c in range(len(WIDTHS)):
        if c > 0:
            early = arrived[c - 1][2], arrived[c - 1][5]
            landed[c] = lax.optimization_barrier((landed[c], *early))[0]
        first, second = unfold(landed[c], sort, half, 1)
        left_first, right_second = shift(first, 1), shift(second, -1)
        left_second, right_first = shift(second, 1), shift(first, -1)
        far_first, far_second = shift(left_first, 1), shift(right_second, -1)
        arrived.append(
            [first, second, left_first, left_second, right_first, right_second, far_first, far_second]
        )
    state = None
    for c in range(len(WIDTHS) - 1):
        early = arrived[c + 1][2], arrived[c + 1][5]
        begun = list(lax.optimization_barrier((*arrived[c], *early))[: len(arrived[c])])
        state = gate_up(begun, gate, up, firsts[c], state, 0, False)
    mine_near = gate_up(arrived[-1][:6], gate, up, firsts[-1], state, 0, True)
    near = [mine_near, shift(mine_near, 1), shift(mine_near, -1), shift(mine_near, 2)]
    mine_far = gate_up(arrived[-1][6:], gate, up, firsts[-1], state, 3, True)
    far = [mine_far, shift(mine_far, 1), shift(mine_far, -1), shift(mine_far, 2)]
    orders = ((0, 1, 2, 3), (2, 0, 3, 1), (1, 3, 0, 2), (3, 2, 1, 0))

    row = jnp.arange(device_count * PAD, dtype=jnp.int32)
    column = jnp.arange(ring * slots, dtype=jnp.int32)
    relative = column // slots
    away = jnp.where(relative == 1, ring - 1, jnp.where(relative == 2, 1, jnp.where(relative == 3, 2, 0)))
    origin = lax.rem(place + away, jnp.int32(ring))
    inner = column % slots
    goal = (inner // capacity * ring + origin) * PAD + inner % capacity
    spread = (row[:, None] == goal[None, :]).astype(jnp.bfloat16)
    complete = down(near, far, down_parts, spread, orders)
    returned = exchange(complete.reshape(device_count, PAD, quarter), None)
    returned = returned.reshape(device_count * PAD, quarter)

    hits = target[:, :, None] == numbers(experts * PAD)[None, None, :]
    mixing = jnp.sum(jnp.where(hits, combine_weight[0][:, :, None], 0.0), axis=1)
    mix_high = lax.reduce_precision(mixing, 8, 7)
    both = jnp.stack([mix_high, mixing - mix_high]).astype(jnp.bfloat16)
    both = both.reshape(2, 1, tok_count, experts, 1, PAD)
    same = jnp.arange(ring)[:, None] == jnp.arange(ring)[None, :]
    both = jnp.where(same[None, :, None, None, :, None], both, jnp.bfloat16(0))
    both = both.reshape(2 * ring * tok_count, device_count * PAD)
    return mix(returned, both, inbound, ring)[None]


def solution(mesh):
    placed = (
        P("section", "expert", None),
        P("section", None),
        P("section", "expert", None),
        P("section", "expert", None),
        P("section", None, "expert"),
        P("section", None, "expert"),
        P("section", "expert", None),
    )
    return jax.shard_map(
        body, mesh=mesh, in_specs=placed, out_specs=P("section", "expert", None), check_vma=False
    )
```

```python
import functools

import jax
import jax.numpy as jnp
from jax import lax
from jax.experimental import pallas as pl
from jax.experimental.pallas import tpu as pltpu
from jax.sharding import PartitionSpec as P

FF_WIN = 1024
HID_DEV = 256
WIDTHS = (4096, 3072)
FOLD = 8
PAD = 8
VMEM = 40 << 20

epsilon = 1e-06


def unfold_kernel(parts, sort_ref, landed_ref, *out_refs):
    cols = landed_ref.shape[1]
    rows = sort_ref.shape[0]
    count = out_refs[0].shape[0]
    halves = len(out_refs) // parts
    for h in range(halves):
        part = landed_ref[h * rows : (h + 1) * rows, :]
        sorted_part = jnp.dot(sort_ref[...], part, preferred_element_type=jnp.float32)
        sorted_part = sorted_part.astype(landed_ref.dtype)
        for q in range(rows // count):
            fold, part_index = q // parts, q % parts
            out_ref = out_refs[part_index * halves + h]
            out_ref[:, fold * cols : (fold + 1) * cols] = sorted_part[q * count : (q + 1) * count]


def unfold(landed, sort, count, parts):
    rows, cols = landed.shape
    halves = rows // sort.shape[0]
    folds = sort.shape[0] // count // parts
    shape = jax.ShapeDtypeStruct((count, cols * folds), landed.dtype)
    return pl.pallas_call(
        functools.partial(unfold_kernel, parts),
        out_shape=[shape] * (halves * parts),
        compiler_params=pltpu.CompilerParams(vmem_limit_bytes=VMEM),
        cost_estimate=pl.CostEstimate(
            flops=2 * rows * cols * sort.shape[0], bytes_accessed=4 * landed.size, transcendentals=0
        ),
        name="unfold",
    )(sort, landed)


def gate_up_kernel(pieces, steps, last, *refs):
    piece_refs = refs[:pieces]
    gate_ref, up_ref = refs[pieces : pieces + 2]
    rest = refs[pieces + 2 :]
    start_refs, out_ref, acc_ref = rest[:-2], rest[-2], rest[-1]
    step = pl.program_id(0)

    @pl.when(step == 0)
    def _():
        if start_refs:
            acc_ref[...] = start_refs[0][...]
        else:
            acc_ref[...] = jnp.zeros_like(acc_ref)

    rows = jnp.concatenate([ref[...] for ref in piece_refs], axis=0)
    hid = gate_ref.shape[1]
    acc_ref[:, :hid] += jnp.dot(rows, gate_ref[...], preferred_element_type=jnp.float32)
    acc_ref[:, hid:] += jnp.dot(rows, up_ref[...], preferred_element_type=jnp.float32)

    @pl.when(step == steps - 1)
    def _():
        if last:
            gate = acc_ref[:, :hid]
            out_ref[...] = (gate / (1.0 + jnp.exp(-gate)) * acc_ref[:, hid:]).astype(out_ref.dtype)
        else:
            out_ref[...] = acc_ref[...]


def gate_up(pieces, gate_weight, up_weight, first_row, before, block, last):
    piece_rows, width = pieces[0].shape
    depth = 1024
    steps = width // depth
    offset = first_row // depth
    rows = piece_rows * len(pieces)
    hid = gate_weight.shape[1]
    start = [] if before is None else [before]
    out_shape = (rows, hid) if last else (rows, 2 * hid)
    out_type = jnp.bfloat16 if last else jnp.float32
    return pl.pallas_call(
        functools.partial(gate_up_kernel, len(pieces), steps, last),
        grid=(steps,),
        in_specs=[pl.BlockSpec((piece_rows, depth), lambda k: (0, k)) for _ in pieces]
        + [pl.BlockSpec((depth, hid), lambda k: (k + offset, 0))] * 2
        + [pl.BlockSpec((rows, 2 * hid), lambda k: (block, 0)) for _ in start],
        out_specs=pl.BlockSpec(out_shape, lambda k: (0, 0)),
        out_shape=jax.ShapeDtypeStruct(out_shape, out_type),
        scratch_shapes=[pltpu.VMEM((rows, 2 * hid), jnp.float32)],
        compiler_params=pltpu.CompilerParams(vmem_limit_bytes=VMEM),
        cost_estimate=pl.CostEstimate(
            flops=4 * rows * hid * width, bytes_accessed=2 * (rows + 2 * hid) * width, transcendentals=0
        ),
        name="gate_up",
    )(*pieces, gate_weight, up_weight, *start)


def down_kernel(orders, *refs):
    parts = len(orders)
    near_refs, far_refs = refs[:parts], refs[parts : 2 * parts]
    weight_refs = refs[2 * parts : 3 * parts]
    spread_ref, out_ref, spread_hid = refs[3 * parts :]
    block, hid = far_refs[0].shape

    @pl.when(pl.program_id(0) == 0)
    def _():
        for j in range(parts):
            blocks = [near_refs[j][b * block : (b + 1) * block, :] for b in range(parts - 1)]
            blocks.append(far_refs[j][...])
            rows = jnp.concatenate([blocks[b] for b in orders[j]], axis=0)
            spread_hid[:, j * hid : (j + 1) * hid] = jnp.dot(
                spread_ref[...], rows, preferred_element_type=jnp.float32
            ).astype(spread_hid.dtype)

    weights = jnp.concatenate([ref[...] for ref in weight_refs], axis=0)
    out_ref[...] = jnp.dot(spread_hid[...], weights, preferred_element_type=jnp.float32).astype(
        out_ref.dtype
    )


def down(near, far, weights, spread, orders):
    hid = far[0].shape[1]
    out_rows, width = spread.shape[0], weights[0].shape[1]
    cols = width // 2
    parts = len(orders)
    return pl.pallas_call(
        functools.partial(down_kernel, orders),
        grid=(width // cols,),
        in_specs=[pl.BlockSpec(near[0].shape, lambda n: (0, 0))] * parts
        + [pl.BlockSpec(far[0].shape, lambda n: (0, 0))] * parts
        + [pl.BlockSpec((hid, cols), lambda n: (0, n))] * parts
        + [pl.BlockSpec(spread.shape, lambda n: (0, 0))],
        out_specs=pl.BlockSpec((out_rows, cols), lambda n: (0, n)),
        out_shape=jax.ShapeDtypeStruct((out_rows, width), jnp.bfloat16),
        scratch_shapes=[pltpu.VMEM((out_rows, parts * hid), jnp.bfloat16)],
        compiler_params=pltpu.CompilerParams(vmem_limit_bytes=VMEM),
        cost_estimate=pl.CostEstimate(
            flops=2 * out_rows * parts * hid * (width + spread.shape[1]),
            bytes_accessed=2 * (out_rows + parts * hid) * width,
            transcendentals=0,
        ),
        name="down",
    )(*near, *far, *weights, spread)


def mix_kernel(parts, width, returned_ref, mixing_ref, inbound_ref, out_ref):
    tokens = inbound_ref.shape[0]
    cols = returned_ref.shape[1]
    start = pl.program_id(0) * cols
    product = jnp.dot(mixing_ref[...], returned_ref[...], preferred_element_type=jnp.float32)
    for f in range(parts):
        at = pl.ds(pl.multiple_of(f * width + start, 128), cols)
        high = product[f * tokens : (f + 1) * tokens]
        low = product[(parts + f) * tokens : (parts + f + 1) * tokens]
        total = inbound_ref[:, at].astype(jnp.float32) + (high + low)
        out_ref[:, at] = total.astype(out_ref.dtype)


def mix(returned, mixing, inbound, parts):
    rows, width = returned.shape
    cols = 896
    return pl.pallas_call(
        functools.partial(mix_kernel, parts, width),
        grid=(width // cols,),
        in_specs=[
            pl.BlockSpec((rows, cols), lambda n: (0, n)),
            pl.BlockSpec(mixing.shape, lambda n: (0, 0)),
            pl.BlockSpec(inbound.shape, lambda n: (0, 0)),
        ],
        out_specs=pl.BlockSpec(inbound.shape, lambda n: (0, 0)),
        out_shape=jax.ShapeDtypeStruct(inbound.shape, inbound.dtype),
        compiler_params=pltpu.CompilerParams(vmem_limit_bytes=VMEM),
        name="mix",
    )(returned, mixing, inbound)


def body(arriving, gains, routes, combine_weight, gate_weight, up_weight, down_weight):
    device_count = lax.axis_size("expert")
    ring = FF_WIN // HID_DEV
    experts = device_count // ring
    tok_count = arriving.shape[1]
    feature_count = arriving.shape[2]
    top_count = routes.shape[2]
    capacity = min(tok_count, 5 * tok_count * top_count // (4 * experts))
    slots = experts * capacity
    half = slots // 2
    quarter = feature_count // ring
    planes = [[g * ring + r for g in range(experts)] for r in range(ring)]
    place = lax.rem(lax.axis_index("expert"), ring)

    def shift(block, step):
        route = [(i, i - i % ring + (i + step) % ring) for i in range(device_count)]
        return lax.ppermute(block, "expert", route)

    def exchange(block, groups):
        return lax.all_to_all(
            block, "expert", split_axis=0, concat_axis=0, axis_index_groups=groups, tiled=True
        )

    def weight_part(step):
        start = lax.rem(place + step, ring) * quarter
        return lax.dynamic_slice_in_dim(down_weight[0], start, quarter, 1)

    def numbers(count):
        return jnp.arange(count, dtype=jnp.int32)

    other = [(i, 1 - i) for i in range(2)]
    inbound = lax.ppermute(arriving, "section", other)[0]
    down_parts = [
        weight_part(0),
        shift(weight_part(1), 1),
        shift(weight_part(3), -1),
        shift(weight_part(2), 2),
    ]
    widened = inbound.astype(jnp.float32)
    inv_rms = lax.rsqrt(jnp.mean(widened * widened, axis=-1, keepdims=True) + epsilon)
    normed = (widened * inv_rms * gains[0][None, :]).astype(jnp.bfloat16)
    chosen = routes[0].reshape(-1)
    onehot = (chosen[:, None] == jnp.arange(experts, dtype=jnp.int32)[None, :]).astype(jnp.int32)
    earlier = jnp.cumsum(onehot, axis=0) - onehot
    slot_index = jnp.sum(earlier * onehot, axis=1)
    target = (chosen * PAD + slot_index).reshape(tok_count, top_count)

    row, token = numbers(experts * FOLD * capacity), numbers(FOLD * tok_count)
    code = row // (FOLD * capacity) * PAD + row % capacity
    hits = jnp.any(jnp.tile(target, (FOLD, 1))[None, :, :] == code[:, None, None], axis=2)
    hits = hits & ((row % (FOLD * capacity) // capacity)[:, None] == (token // tok_count)[None, :])
    placement = hits.astype(jnp.bfloat16)
    packed, firsts = [], []
    for width in WIDTHS:
        firsts.append(firsts[-1] + WIDTHS[len(firsts) - 1] if firsts else 0)
        cols = width // FOLD
        cuts = [firsts[-1] + f * cols for f in range(FOLD)]
        folded = jnp.concatenate([normed[:, cut : cut + cols] for cut in cuts], axis=0)
        block = jnp.dot(placement, folded, preferred_element_type=jnp.float32)
        packed.append(block.astype(jnp.bfloat16).reshape(experts, FOLD * capacity, cols))

    to_row, from_row = numbers(FOLD * half), numbers(FOLD * half)
    wanted = to_row % half // capacity * (FOLD * capacity) + to_row // half * capacity + to_row % capacity
    sort = (wanted[:, None] == from_row[None, :]).astype(jnp.bfloat16)

    gate, up = gate_weight[0], up_weight[0]
    packed[1], *down_parts = lax.optimization_barrier((packed[1], *down_parts))
    landed = [exchange(block, planes) for block in packed]
    landed = [block.reshape(FOLD * slots, block.shape[2]) for block in landed]
    arrived = []
    for c in range(len(WIDTHS)):
        first, second = unfold(landed[c], sort, half, 1)
        left_first, right_second = shift(first, 1), shift(second, -1)
        left_second, right_first = shift(second, 1), shift(first, -1)
        far_first, far_second = shift(left_first, 1), shift(right_second, -1)
        arrived.append(
            [first, second, left_first, left_second, right_first, right_second, far_first, far_second]
        )
    state = None
    for c in range(len(WIDTHS) - 1):
        state = gate_up(arrived[c], gate, up, firsts[c], state, 0, False)
    mine_near = gate_up(arrived[-1][:6], gate, up, firsts[-1], state, 0, True)
    near = [mine_near, shift(mine_near, 1), shift(mine_near, -1), shift(mine_near, 2)]
    mine_far = gate_up(arrived[-1][6:], gate, up, firsts[-1], state, 3, True)
    far = [mine_far, shift(mine_far, 1), shift(mine_far, -1), shift(mine_far, 2)]
    orders = ((0, 1, 2, 3), (2, 0, 3, 1), (1, 3, 0, 2), (3, 2, 1, 0))

    row = jnp.arange(device_count * PAD, dtype=jnp.int32)
    column = jnp.arange(ring * slots, dtype=jnp.int32)
    relative = column // slots
    away = jnp.where(relative == 1, ring - 1, jnp.where(relative == 2, 1, jnp.where(relative == 3, 2, 0)))
    origin = lax.rem(place + away, jnp.int32(ring))
    inner = column % slots
    goal = (inner // capacity * ring + origin) * PAD + inner % capacity
    spread = (row[:, None] == goal[None, :]).astype(jnp.bfloat16)
    complete = down(near, far, down_parts, spread, orders)
    returned = exchange(complete.reshape(device_count, PAD, quarter), None)
    returned = returned.reshape(device_count * PAD, quarter)

    hits = target[:, :, None] == numbers(experts * PAD)[None, None, :]
    mixing = jnp.sum(jnp.where(hits, combine_weight[0][:, :, None], 0.0), axis=1)
    mix_high = lax.reduce_precision(mixing, 8, 7)
    both = jnp.stack([mix_high, mixing - mix_high]).astype(jnp.bfloat16)
    both = both.reshape(2, 1, tok_count, experts, 1, PAD)
    same = jnp.arange(ring)[:, None] == jnp.arange(ring)[None, :]
    both = jnp.where(same[None, :, None, None, :, None], both, jnp.bfloat16(0))
    both = both.reshape(2 * ring * tok_count, device_count * PAD)
    return mix(returned, both, inbound, ring)[None]


def solution(mesh):
    placed = (
        P("section", "expert", None),
        P("section", None),
        P("section", "expert", None),
        P("section", "expert", None),
        P("section", None, "expert"),
        P("section", None, "expert"),
        P("section", "expert", None),
    )
    return jax.shard_map(
        body, mesh=mesh, in_specs=placed, out_specs=P("section", "expert", None), check_vma=False
    )
```
